32 devices in a mesh: dp: 4 (over z), shard: 8 (over y, x, core).
Axes of the slice: x: 2, y: 2, z: 4, core: 2. Of those that a mesh axis runs over, the one named last changes fastest.
Arguments:
- hidden_in: bfloat16 [4096, 5120], P('dp', 'shard'), may hold values from -6 to 6
- context_in: bfloat16 [4096, 5120], P('dp', 'shard'), may hold values from -6 to 6
- query_cotan: bfloat16 [4096, 2560], P('dp', 'shard'), may hold values from -0.1875 to 0.1875
- output_cotan: bfloat16 [4096, 2560], P('dp', 'shard'), may hold values from -0.1875 to 0.1875
- query_error: bfloat16 [4, 5120, 2560], P('dp', 'shard'), may hold values from -3 to 3
- output_error: bfloat16 [4, 5120, 2560], P('dp', 'shard'), may hold values from -3 to 3
- query_weight: float32 [5120, 2560], P('shard', 'dp'), may hold values from -0.6 to 0.6
- output_weight: float32 [5120, 2560], P('shard', 'dp'), may hold values from -0.6 to 0.6
- start_factors: bfloat16 [2, 2560, 32], replicated, may hold values from -0.09863281 to 0.09863281
Outputs:
- query_error_new: bfloat16 [4, 5120, 2560], P('dp', 'shard')
- output_error_new: bfloat16 [4, 5120, 2560], P('dp', 'shard')
- query_weight_new: float32 [5120, 2560], P('shard', 'dp')
- output_weight_new: float32 [5120, 2560], P('shard', 'dp')
The draws below stay inside these ranges and needn't reach their ends.
All inputs are finite; a program needn't handle non-finite values.
Results may differ from the reference program's by a relative error of at most 0.005.
Values may be sent and summed in bfloat16 or wider, within the bound.
A program may use at most 128 MiB of HBM per device.

```python
import jax
import jax.numpy as jnp
from jax import lax

D = 5120
DOUT = 2560
RANK = 32
TOK = 1024
TOKENS = 4096
N_DP = 4


def block_scale(stream_key, dims, split, smallest, top_value):
    def one(position, shards_of):
        heights = jax.random.uniform(jax.random.fold_in(jax.random.fold_in(stream_key, 6), position), (shards_of,), jnp.float32, smallest / len(split), top_value / len(split))
        return jnp.repeat(jnp.exp(heights), dims[position] // shards_of).reshape((-1,) + (1,) * (len(dims) - position - 1))

    gain = one(*split[0])
    for cut in split[1:]:
        gain = gain * one(*cut)
    return gain


def scatter_about(rng, extent, width, limit, cuts=(), held_as=jnp.bfloat16):
    entries = width * jax.random.normal(rng, extent, jnp.float32)
    if cuts:
        entries = entries * block_scale(rng, extent, cuts, -0.22, 0.18)
    return jnp.clip(entries, -limit, limit).astype(held_as)


def setup_inputs(seed: int = 0) -> dict:
    key_list = jax.random.split(jax.random.key(seed), 10)
    hidden_in = scatter_about(key_list[0], (TOKENS, D), 1.0, 6.0, ((0, 4), (1, 8)))
    context_in = scatter_about(key_list[1], (TOKENS, D), 1.0, 6.0, ((0, 4), (1, 8)))
    query_cotan = scatter_about(key_list[2], (TOKENS, DOUT), (TOK ** -0.5), 0.1875, ((0, 4), (1, 8)))
    output_cotan = scatter_about(key_list[3], (TOKENS, DOUT), (TOK ** -0.5), 0.1875, ((0, 4), (1, 8)))
    query_error = scatter_about(key_list[4], (N_DP, D, DOUT), 0.5, 3.0, ((0, 4), (1, 8)))
    output_error = scatter_about(key_list[5], (N_DP, D, DOUT), 0.5, 3.0, ((0, 4), (1, 8)))
    query_weight = scatter_about(key_list[6], (D, DOUT), 0.1, 0.6, ((0, 8), (1, 4)), jnp.float32)
    output_weight = scatter_about(key_list[7], (D, DOUT), 0.1, 0.6, ((0, 8), (1, 4)), jnp.float32)
    start_factors = scatter_about(key_list[8], (2, DOUT, RANK), (DOUT ** -0.5), 0.09863281)
    return {"hidden_in": hidden_in, "context_in": context_in, "query_cotan": query_cotan, "output_cotan": output_cotan, "query_error": query_error, "output_error": output_error, "query_weight": query_weight, "output_weight": output_weight, "start_factors": start_factors}


HIGH = lax.Precision.HIGHEST

def compress(inputs, cotan, error, weight, start):
    acts = inputs.reshape(N_DP, TOK, D)
    grads = cotan.reshape(N_DP, TOK, DOUT)
    start32 = start.astype(jnp.float32)

    def form(index):
        grad = lax.dot_general(acts[index].astype(jnp.float32), grads[index].astype(jnp.float32), (((0,), (0,)), ((), ())), preferred_element_type=jnp.float32)
        return grad + error[index].astype(jnp.float32)
    full = lax.map(form, jnp.arange(N_DP, dtype=jnp.int32))
    left = jnp.einsum('rdo,ok->dk', full, start32, precision=HIGH) / jnp.float32(N_DP)
    gram = jnp.dot(left.T, left, precision=HIGH)
    chol = jnp.linalg.cholesky(gram)
    ortho = lax.linalg.triangular_solve(chol, left, left_side=False, lower=True, transpose_a=True)
    right = jnp.einsum('rdo,dk->ok', full, ortho, precision=HIGH) / jnp.float32(N_DP)
    approx = jnp.dot(ortho, right.T, precision=HIGH)
    error_new = (full - approx[None]).astype(jnp.bfloat16)
    return (error_new, weight - approx)

def reference(hidden_in, context_in, query_cotan, output_cotan, query_error, output_error, query_weight, output_weight, start_factors):
    query_error_new, query_weight_new = compress(hidden_in, query_cotan, query_error, query_weight, start_factors[0])
    output_error_new, output_weight_new = compress(context_in, output_cotan, output_error, output_weight, start_factors[1])
    return (query_error_new, output_error_new, query_weight_new, output_weight_new)
```

```python
import functools

import jax
import jax.numpy as jnp
from jax import lax
from jax.experimental import pallas as pl
from jax.experimental.pallas import tpu as pltpu
from jax.sharding import PartitionSpec as P

HIGH = lax.Precision.HIGHEST


def contract_tokens(left_op, right_op):
    return lax.dot_general(
        left_op, right_op, (((0,), (0,)), ((), ())), preferred_element_type=jnp.float32
    )


def form_grads(hidden_in, context_in, query_cotan, output_cotan):

    def query_part(piece, start):
        return contract_tokens(hidden_in, piece)

    def output_part(piece, start):
        return contract_tokens(context_in, piece)

    query_grad = query_part(lax.all_gather(query_cotan, "shard", axis=1, tiled=True), jnp.int32(0))
    output_grad = output_part(
        lax.all_gather(output_cotan, "shard", axis=1, tiled=True), jnp.int32(0)
    )
    return (query_grad, output_grad)


def orthonormal(left, gram):
    chol = jnp.linalg.cholesky(gram)
    return lax.linalg.triangular_solve(chol, left, left_side=False, lower=True, transpose_a=True)


def body(
    hidden_in,
    context_in,
    query_cotan,
    output_cotan,
    query_error,
    output_error,
    query_weight,
    output_weight,
    start_factors,
):
    replicas = lax.axis_size("dp")
    query_start = start_factors[0].astype(jnp.float32)
    output_start = start_factors[1].astype(jnp.float32)
    query_prior = query_error[0].astype(jnp.float32)
    output_prior = output_error[0].astype(jnp.float32)
    query_grad, output_grad = form_grads(hidden_in, context_in, query_cotan, output_cotan)
    query_full = query_grad + query_prior
    output_full = output_grad + output_prior
    query_left = jnp.dot(query_full, query_start, precision=HIGH)
    output_left = jnp.dot(output_full, output_start, precision=HIGH)
    query_left, output_left = lax.psum((query_left, output_left), "dp")
    query_left = query_left / jnp.float32(replicas)
    output_left = output_left / jnp.float32(replicas)
    query_gram, output_gram = lax.psum(
        (
            jnp.dot(query_left.T, query_left, precision=HIGH),
            jnp.dot(output_left.T, output_left, precision=HIGH),
        ),
        "shard",
    )
    query_ortho = orthonormal(query_left, query_gram)
    output_ortho = orthonormal(output_left, output_gram)
    query_term = jnp.dot(query_full.T, query_ortho, precision=HIGH)
    output_term = jnp.dot(output_full.T, output_ortho, precision=HIGH)
    query_part, output_part = (
        lax.psum_scatter(
            query_term.astype(jnp.bfloat16), "shard", scatter_dimension=0, tiled=True
        ).astype(jnp.float32),
        lax.psum_scatter(
            output_term.astype(jnp.bfloat16), "shard", scatter_dimension=0, tiled=True
        ).astype(jnp.float32),
    )
    query_part, output_part = lax.psum((query_part, output_part), "dp")
    query_right, output_right = (
        lax.all_gather(query_part, "shard", axis=0, tiled=True),
        lax.all_gather(output_part, "shard", axis=0, tiled=True),
    )
    query_right = query_right / jnp.float32(replicas)
    output_right = output_right / jnp.float32(replicas)
    query_approx = jnp.dot(query_ortho, query_right.T, precision=HIGH)
    output_approx = jnp.dot(output_ortho, output_right.T, precision=HIGH)
    query_error_new = (query_full - query_approx).astype(jnp.bfloat16)[None]
    output_error_new = (output_full - output_approx).astype(jnp.bfloat16)[None]
    weight_cols = query_weight.shape[1]
    col_start = lax.axis_index("dp") * weight_cols
    query_cols = lax.dynamic_slice_in_dim(query_approx, col_start, weight_cols, 1)
    output_cols = lax.dynamic_slice_in_dim(output_approx, col_start, weight_cols, 1)
    return (
        query_error_new,
        output_error_new,
        query_weight - query_cols,
        output_weight - output_cols,
    )


NT = (((1,), (1,)), ((), ()))
NN = (((1,), (0,)), ((), ()))
TN = (((0,), (0,)), ((), ()))
MESH = pl.DeviceIdType.MESH


def mxu(lhs, rhs, dims):
    return lax.dot_general(lhs, rhs, dims, preferred_element_type=jnp.float32)


def two_terms(value):
    high = value.astype(jnp.bfloat16)
    low = (value - high.astype(jnp.float32)).astype(jnp.bfloat16)
    return jnp.concatenate([high, low], axis=0)


def split_dot(value, rhs, dims):
    rows = value.shape[0]
    both = mxu(two_terms(value), rhs, dims)
    return both[:rows] + both[rows:]


def spd_inverse(gram):
    size = gram.shape[0]
    row_id = lax.broadcasted_iota(jnp.int32, (size, size), 0)
    col_id = lax.broadcasted_iota(jnp.int32, (size, size), 1)
    value = gram
    for k in range(size):
        row = value[k : k + 1, :]
        col = value[:, k : k + 1]
        inv = 1.0 / value[k : k + 1, k : k + 1]
        scaled = row * inv
        rest = value - col * scaled
        rest = jnp.where(col_id == k, -col * inv, rest)
        value = jnp.where(row_id == k, jnp.where(col_id == k, inv, scaled), rest)
    return value


def chain_kernel(
    n, reps,
    a0_hbm, a1_hbm, b0, b1, e0_hbm, e1_hbm, st, sloc,
    g0, g1, at0, at1, lg, rf,
    a0, a1, e0, e1, ps, pr, pf, ls, lr, lf, qs, qr, qf, ts, tr, gs, gr, rs, rr, rd,
    load_sem, own_send, own_recv, fwd_send, fwd_recv, core_send, core_recv,
    ps_s, ps_r, pg_s, pg_r, ls_s, ls_r, lg_s, lg_r,
    qs_s, qs_r, qg_s, qg_r, ts_s, ts_r, gs_s, gs_r,
    rs_s, rs_r, rg_s, rg_r, rf_s, rf_r,
):
    me = lax.axis_index("shard")
    z = lax.axis_index("dp")
    rank = st.shape[1]
    rows = 2 * rank // reps
    acts, errs, cots, gathered = (a0, a1), (e0, e1), (b0, b1), (g0, g1)
    half = b0.shape[0] // 2

    loads = [
        pltpu.make_async_copy(src, dst, load_sem.at[i])
        for i, (src, dst) in enumerate(
            ((e0_hbm, e0), (e1_hbm, e1), (a0_hbm, a0), (a1_hbm, a1), (b0, g0.at[me]), (b1, g1.at[me]))
        )
    ]
    for load in loads:
        load.start()

    barrier = pltpu.get_barrier_semaphore()
    for k in range(1, n):
        pl.semaphore_signal(barrier, inc=1, device_id=(z, lax.rem(me + k, n)), device_id_type=MESH)
    for k in range(1, reps):
        pl.semaphore_signal(barrier, inc=1, device_id=(lax.rem(z + k, reps), me), device_id_type=MESH)
    pl.semaphore_wait(barrier, n - 1 + reps - 1)

    def remote(src, dst, ss, rsem, target):
        return pltpu.make_async_remote_copy(
            src_ref=src, dst_ref=dst, send_sem=ss, recv_sem=rsem,
            device_id=target, device_id_type=MESH,
        )

    def shard_peer(k):
        return (z, lax.rem(me + k, n))

    def dp_peer(k):
        return (lax.rem(z + k, reps), me)

    def start(copies):
        for copy in copies:
            copy.start()
        return copies

    def arrived(copies):
        for copy in copies:
            copy.wait_recv()

    def scatter(src, dst, ss, rsem):
        return start([
            remote(src.at[lax.rem(me + k, n)], dst.at[k - 1], ss.at[k - 1], rsem.at[k - 1], shard_peer(k))
            for k in range(1, n)
        ])

    def spread(buf, ss, rsem):
        return start([
            remote(buf.at[me], buf.at[me], ss.at[k - 1], rsem.at[k - 1], shard_peer(k))
            for k in range(1, n)
        ])

    def total(own, parts, count):
        value = own
        for k in range(count):
            value = value + parts[k].astype(jnp.float32)
        return value

    def dp_scatter(src, dst, ss, rsem):
        return start([
            remote(
                src.at[pl.ds(pl.multiple_of(lax.rem(z + k, reps) * rows, rows), rows)],
                dst.at[k - 1], ss.at[k - 1], rsem.at[k - 1], dp_peer(k),
            )
            for k in range(1, reps)
        ])

    mine = pl.ds(pl.multiple_of(z * rows, rows), rows)

    def dp_spread(buf, ss, rsem):
        return start([
            remote(buf.at[mine], buf.at[mine], ss.at[k - 1], rsem.at[k - 1], dp_peer(k))
            for k in range(1, reps)
        ])

    c = lax.rem(me, 2)
    x = lax.rem(me // 2, 2)
    y = me // 4
    at_c = me + 1 - 2 * c
    at_x = me + 2 - 4 * x
    at_y = me + 4 - 8 * y
    at_d = at_x + 4 - 8 * y
    pending = []

    token_piece = ps.shape[2]
    for p in range(2):
        value = mxu(sloc[p], cots[p][...], NT)
        for j in range(n):
            ps[j, rank * p : rank * (p + 1), :] = value[:, j * token_piece : (j + 1) * token_piece]
    sent = scatter(ps, pr, ps_s, ps_r)
    pending += sent

    own = []
    for p in range(2):
        for i, target in enumerate((at_x, at_y, at_c)):
            own.append(remote(
                cots[p], gathered[p].at[me], own_send.at[3 * p + i], own_recv.at[3 * p + i], (z, target)
            ))
    start(own)
    pending += own

    loads[0].wait()
    loads[1].wait()
    prior = [mxu(st[p], errs[p][...], NT) for p in range(2)]

    arrived(sent)
    pf[me] = total(ps[me], pr, n - 1)
    sent = spread(pf, pg_s, pg_r)
    pending += sent
    loads[2].wait()
    loads[3].wait()
    arrived(sent)
    for p in range(2):
        value = jnp.concatenate([pf[j, rank * p : rank * (p + 1), :] for j in range(n)], axis=1)
        ls[rank * p : rank * (p + 1), :] = split_dot(value, acts[p][...], NN) + prior[p]
    sent = dp_scatter(ls, lr, ls_s, ls_r)
    pending += sent
    at0[...] = a0[...].T
    arrived(sent)
    lf[mine, :] = total(ls[mine, :], lr, reps - 1) * (1.0 / reps)
    sent = dp_spread(lf, lg_s, lg_r)
    pending += sent
    at1[...] = a1[...].T
    arrived(sent)

    lefts = [lf[rank * p : rank * (p + 1), :] for p in range(2)]
    for p in range(2):
        value = split_dot(lefts[p], acts[p][...], NT)
        for j in range(n):
            qs[j, rank * p : rank * (p + 1), :] = value[:, j * token_piece : (j + 1) * token_piece]
    q_sent = scatter(qs, qr, qs_s, qs_r)
    gs[...] = jnp.zeros_like(gs)
    for p in range(2):
        gs[p, :, 0:rank] = lax.dot_general(
            lefts[p], lefts[p], NT, precision=HIGH, preferred_element_type=jnp.float32
        )
    g_sent = start([
        remote(gs, gr.at[k - 1], gs_s.at[k - 1], gs_r.at[k - 1], shard_peer(k)) for k in range(1, n)
    ])
    cols = ts.shape[2]
    for p in range(2):
        value = split_dot(lefts[p], errs[p][...], NN).astype(jnp.bfloat16)
        for j in range(n):
            ts[j, rank * p : rank * (p + 1), :] = value[:, j * cols : (j + 1) * cols]
    t_sent = scatter(ts, tr, ts_s, ts_r)
    pending += q_sent + g_sent + t_sent

    arrived(q_sent)
    qf[me] = total(qs[me], qr, n - 1)
    sent = spread(qf, qg_s, qg_r)
    pending += sent

    forwards, to_core = [], []
    for p in range(2):
        own[3 * p].wait_recv()
        own[3 * p + 1].wait_recv()
        top, low = pl.ds(0, half), pl.ds(half, half)
        via_y = gathered[p].at[at_x, top]
        via_x = gathered[p].at[at_y, low]
        pair = start([
            remote(via_y, via_y, fwd_send.at[2 * p], fwd_recv.at[2 * p], (z, at_y)),
            remote(via_x, via_x, fwd_send.at[2 * p + 1], fwd_recv.at[2 * p + 1], (z, at_x)),
        ])
        forwards += pair
        to_core += start([
            remote(gathered[p].at[at_x], gathered[p].at[at_x], core_send.at[4 * p], core_recv.at[4 * p], (z, at_c)),
            remote(gathered[p].at[at_y], gathered[p].at[at_y], core_send.at[4 * p + 1], core_recv.at[4 * p + 1], (z, at_c)),
        ])

    arrived(sent)
    arrived(t_sent)
    for p in range(2):
        part = pl.ds(rank * p, rank)
        value = jnp.concatenate([qf[j, rank * p : rank * (p + 1), :] for j in range(n)], axis=1)
        value = split_dot(value, cots[p][...], NN) + ts[me, part, :].astype(jnp.float32)
        for k in range(n - 1):
            value = value + tr[k, part, :].astype(jnp.float32)
        rs[part, :] = value
    sent = dp_scatter(rs, rr, rs_s, rs_r)
    pending += sent
    arrived(g_sent)
    arrived(sent)
    rd[mine, :] = total(rs[mine, :], rr, reps - 1) * (1.0 / reps)
    sent = dp_spread(rd, rg_s, rg_r)
    pending += sent
    arrived(sent)
    rf[me] = rd[...].astype(jnp.bfloat16)
    sent = spread(rf, rf_s, rf_r)
    pending += sent
    grams = [total(gs[p, :, 0:rank], [gr[k, p, :, 0:rank] for k in range(n - 1)], n - 1) for p in range(2)]
    for p in range(2):
        lg[rank * p : rank * (p + 1), :] = lax.dot_general(
            spd_inverse(grams[p]), lefts[p], NN, precision=HIGH, preferred_element_type=jnp.float32
        )
    for p in range(2):
        forwards[2 * p].wait_recv()
        forwards[2 * p + 1].wait_recv()
        top, low = pl.ds(0, half), pl.ds(half, half)
        to_core += start([
            remote(gathered[p].at[at_d, part], gathered[p].at[at_d, part],
                   core_send.at[4 * p + 2 + i], core_recv.at[4 * p + 2 + i], (z, at_c))
            for i, part in enumerate((top, low))
        ])
    arrived(sent)
    arrived(to_core)
    own[2].wait_recv()
    own[5].wait_recv()
    for copy in pending + forwards + to_core:
        copy.wait_send()
    loads[4].wait()
    loads[5].wait()


def final_kernel(p, at, b, e, lg, rf, w, e_new, w_new):
    rank = lg.shape[0] // 2
    step = pl.program_id(0)
    part = slice(rank * p, rank * (p + 1))
    columns = jnp.concatenate([b[0], b[1]], axis=1)
    right = jnp.concatenate([rf[0, part, :], rf[1, part, :]], axis=1)
    approx = mxu(two_terms(lg[part, :]), jnp.concatenate([right, right], axis=0), TN)
    full = mxu(at[...], columns, NN) + e[0].astype(jnp.float32)
    e_new[0] = (full - approx).astype(jnp.bfloat16)

    @pl.when(step == lax.axis_index("dp"))
    def _():
        w_new[...] = w[...] - approx


def fast_body(
    hidden_in, context_in, query_cotan, output_cotan,
    query_error, output_error, query_weight, output_weight, start_factors,
):
    n = lax.axis_size("shard")
    reps = lax.axis_size("dp")
    tok, width = hidden_in.shape
    cols = query_cotan.shape[1]
    dout = start_factors.shape[1]
    rank = start_factors.shape[2]
    f32, bf16 = jnp.float32, jnp.bfloat16
    st = jnp.swapaxes(start_factors, 1, 2)
    sloc = jnp.swapaxes(
        lax.dynamic_slice_in_dim(start_factors, lax.axis_index("shard") * cols, cols, 1), 1, 2
    )
    any_spec = pl.BlockSpec(memory_space=pl.ANY)
    vmem = pl.BlockSpec(memory_space=pltpu.VMEM)
    dma = pltpu.SemaphoreType.DMA
    piece = tok // n
    rows = 2 * rank // reps
    wide = 2 * rank
    g0, g1, at0, at1, lg, rf = pl.pallas_call(
        functools.partial(chain_kernel, n, reps),
        out_shape=(
            jax.ShapeDtypeStruct((n, tok, cols), bf16),
            jax.ShapeDtypeStruct((n, tok, cols), bf16),
            jax.ShapeDtypeStruct((width, tok), bf16),
            jax.ShapeDtypeStruct((width, tok), bf16),
            jax.ShapeDtypeStruct((wide, width), f32),
            jax.ShapeDtypeStruct((n, wide, cols), bf16),
        ),
        in_specs=[any_spec, any_spec, vmem, vmem, any_spec, any_spec, vmem, vmem],
        out_specs=(any_spec, any_spec, vmem, vmem, vmem, vmem),
        scratch_shapes=[
            pltpu.VMEM((tok, width), bf16),
            pltpu.VMEM((tok, width), bf16),
            pltpu.VMEM((width, dout), bf16),
            pltpu.VMEM((width, dout), bf16),
            pltpu.VMEM((n, wide, piece), f32),
            pltpu.VMEM((n - 1, wide, piece), f32),
            pltpu.VMEM((n, wide, piece), f32),
            pltpu.VMEM((wide, width), f32),
            pltpu.VMEM((reps - 1, rows, width), f32),
            pltpu.VMEM((wide, width), f32),
            pltpu.VMEM((n, wide, piece), f32),
            pltpu.VMEM((n - 1, wide, piece), f32),
            pltpu.VMEM((n, wide, piece), f32),
            pltpu.VMEM((n, wide, cols), bf16),
            pltpu.VMEM((n - 1, wide, cols), bf16),
            pltpu.VMEM((2, rank, 128), f32),
            pltpu.VMEM((n - 1, 2, rank, 128), f32),
            pltpu.VMEM((wide, cols), f32),
            pltpu.VMEM((reps - 1, rows, cols), f32),
            pltpu.VMEM((wide, cols), f32),
            dma((6,)), dma((6,)), dma((6,)), dma((4,)), dma((4,)), dma((8,)), dma((8,)),
        ]
        + [dma((n - 1,))] * 4 + [dma((reps - 1,))] * 4
        + [dma((n - 1,))] * 8 + [dma((reps - 1,))] * 4 + [dma((n - 1,))] * 2,
        compiler_params=pltpu.CompilerParams(
            collective_id=0, has_side_effects=True, vmem_limit_bytes=48 * 1024 * 1024
        ),
    )(
        hidden_in, context_in, query_cotan, output_cotan,
        query_error[0], output_error[0], st, sloc,
    )

    span = 2 * cols

    def final(p, at, gathered, error, weight):
        return pl.pallas_call(
            functools.partial(final_kernel, p),
            grid=(dout // span,),
            in_specs=[
                pl.BlockSpec((width, tok), lambda i: (0, 0)),
                pl.BlockSpec((2, tok, cols), lambda i: (i, 0, 0)),
                pl.BlockSpec((1, width, span), lambda i: (0, 0, i)),
                pl.BlockSpec((wide, width), lambda i: (0, 0)),
                pl.BlockSpec((2, wide, cols), lambda i: (i, 0, 0)),
                pl.BlockSpec((width, span), lambda i: (0, 0)),
            ],
            out_specs=(
                pl.BlockSpec((1, width, span), lambda i: (0, 0, i)),
                pl.BlockSpec((width, span), lambda i: (0, 0)),
            ),
            out_shape=(
                jax.ShapeDtypeStruct(error.shape, error.dtype),
                jax.ShapeDtypeStruct(weight.shape, weight.dtype),
            ),
            compiler_params=pltpu.CompilerParams(vmem_limit_bytes=48 * 1024 * 1024),
        )(at, gathered, error, lg, rf, weight)

    query_error_new, query_weight_new = final(0, at0, g0, query_error, query_weight)
    output_error_new, output_weight_new = final(1, at1, g1, output_error, output_weight)
    return (query_error_new, output_error_new, query_weight_new, output_weight_new)


def solution(mesh):
    placed = (
        P("dp", "shard"),
        P("dp", "shard"),
        P("dp", "shard"),
        P("dp", "shard"),
        P("dp", "shard", None),
        P("dp", "shard", None),
        P("shard", "dp"),
        P("shard", "dp"),
        P(),
    )
    return jax.shard_map(
        fast_body if mesh.shape["shard"] == 8 and mesh.shape["dp"] == 4 else body,
        mesh=mesh,
        in_specs=placed,
        out_specs=(
            P("dp", "shard", None),
            P("dp", "shard", None),
            P("shard", "dp"),
            P("shard", "dp"),
        ),
        check_vma=False,
    )
```

```python
import functools

import jax
import jax.numpy as jnp
from jax import lax
from jax.experimental import pallas as pl
from jax.experimental.pallas import tpu as pltpu
from jax.sharding import PartitionSpec as P

HIGH = lax.Precision.HIGHEST


def contract_tokens(left_op, right_op):
    return lax.dot_general(
        left_op, right_op, (((0,), (0,)), ((), ())), preferred_element_type=jnp.float32
    )


def form_grads(hidden_in, context_in, query_cotan, output_cotan):

    def query_part(piece, start):
        return contract_tokens(hidden_in, piece)

    def output_part(piece, start):
        return contract_tokens(context_in, piece)

    query_grad = query_part(lax.all_gather(query_cotan, "shard", axis=1, tiled=True), jnp.int32(0))
    output_grad = output_part(
        lax.all_gather(output_cotan, "shard", axis=1, tiled=True), jnp.int32(0)
    )
    return (query_grad, output_grad)


def orthonormal(left, gram):
    chol = jnp.linalg.cholesky(gram)
    return lax.linalg.triangular_solve(chol, left, left_side=False, lower=True, transpose_a=True)


def body(
    hidden_in,
    context_in,
    query_cotan,
    output_cotan,
    query_error,
    output_error,
    query_weight,
    output_weight,
    start_factors,
):
    replicas = lax.axis_size("dp")
    query_start = start_factors[0].astype(jnp.float32)
    output_start = start_factors[1].astype(jnp.float32)
    query_prior = query_error[0].astype(jnp.float32)
    output_prior = output_error[0].astype(jnp.float32)
    query_grad, output_grad = form_grads(hidden_in, context_in, query_cotan, output_cotan)
    query_full = query_grad + query_prior
    output_full = output_grad + output_prior
    query_left = jnp.dot(query_full, query_start, precision=HIGH)
    output_left = jnp.dot(output_full, output_start, precision=HIGH)
    query_left, output_left = lax.psum((query_left, output_left), "dp")
    query_left = query_left / jnp.float32(replicas)
    output_left = output_left / jnp.float32(replicas)
    query_gram, output_gram = lax.psum(
        (
            jnp.dot(query_left.T, query_left, precision=HIGH),
            jnp.dot(output_left.T, output_left, precision=HIGH),
        ),
        "shard",
    )
    query_ortho = orthonormal(query_left, query_gram)
    output_ortho = orthonormal(output_left, output_gram)
    query_term = jnp.dot(query_full.T, query_ortho, precision=HIGH)
    output_term = jnp.dot(output_full.T, output_ortho, precision=HIGH)
    query_part, output_part = (
        lax.psum_scatter(
            query_term.astype(jnp.bfloat16), "shard", scatter_dimension=0, tiled=True
        ).astype(jnp.float32),
        lax.psum_scatter(
            output_term.astype(jnp.bfloat16), "shard", scatter_dimension=0, tiled=True
        ).astype(jnp.float32),
    )
    query_part, output_part = lax.psum((query_part, output_part), "dp")
    query_right, output_right = (
        lax.all_gather(query_part, "shard", axis=0, tiled=True),
        lax.all_gather(output_part, "shard", axis=0, tiled=True),
    )
    query_right = query_right / jnp.float32(replicas)
    output_right = output_right / jnp.float32(replicas)
    query_approx = jnp.dot(query_ortho, query_right.T, precision=HIGH)
    output_approx = jnp.dot(output_ortho, output_right.T, precision=HIGH)
    query_error_new = (query_full - query_approx).astype(jnp.bfloat16)[None]
    output_error_new = (output_full - output_approx).astype(jnp.bfloat16)[None]
    weight_cols = query_weight.shape[1]
    col_start = lax.axis_index("dp") * weight_cols
    query_cols = lax.dynamic_slice_in_dim(query_approx, col_start, weight_cols, 1)
    output_cols = lax.dynamic_slice_in_dim(output_approx, col_start, weight_cols, 1)
    return (
        query_error_new,
        output_error_new,
        query_weight - query_cols,
        output_weight - output_cols,
    )


NT = (((1,), (1,)), ((), ()))
NN = (((1,), (0,)), ((), ()))
TN = (((0,), (0,)), ((), ()))
MESH = pl.DeviceIdType.MESH


def mxu(lhs, rhs, dims):
    return lax.dot_general(lhs, rhs, dims, preferred_element_type=jnp.float32)


def two_terms(value):
    high = value.astype(jnp.bfloat16)
    low = (value - high.astype(jnp.float32)).astype(jnp.bfloat16)
    return jnp.concatenate([high, low], axis=0)


def split_dot(value, rhs, dims):
    rows = value.shape[0]
    both = mxu(two_terms(value), rhs, dims)
    return both[:rows] + both[rows:]


def spd_inverse(gram):
    size = gram.shape[0]
    row_id = lax.broadcasted_iota(jnp.int32, (size, size), 0)
    col_id = lax.broadcasted_iota(jnp.int32, (size, size), 1)
    value = gram
    for k in range(size):
        row = value[k : k + 1, :]
        col = value[:, k : k + 1]
        inv = 1.0 / value[k : k + 1, k : k + 1]
        scaled = row * inv
        rest = value - col * scaled
        rest = jnp.where(col_id == k, -col * inv, rest)
        value = jnp.where(row_id == k, jnp.where(col_id == k, inv, scaled), rest)
    return value


def chain_kernel(
    n, reps,
    a0_hbm, a1_hbm, b0, b1, e0_hbm, e1_hbm, st, sloc,
    g0, g1, at0, at1, lg, right,
    bt0, bt1, rf, a0, a1, e0, e1, ps, pr, pf, ls, lr, lf, qs, qr, qf, ts, tr, gs, gr, rs, rr, rd,
    load_sem, own_send, own_recv, fwd_send, fwd_recv, core_send, core_recv,
    ps_s, ps_r, pg_s, pg_r, ls_s, ls_r, lg_s, lg_r,
    qs_s, qs_r, qg_s, qg_r, ts_s, ts_r, gs_s, gs_r,
    rs_s, rs_r, rg_s, rg_r, rf_s, rf_r,
):
    me = lax.axis_index("shard")
    z = lax.axis_index("dp")
    rank = st.shape[1]
    acts, errs, cots, gathered = (a0, a1), (e0, e1), (bt0, bt1), (g0, g1)
    half = b0.shape[1] // 2

    loads = [
        pltpu.make_async_copy(src, dst, load_sem.at[i])
        for i, (src, dst) in enumerate(
            ((e0_hbm, e0), (e1_hbm, e1), (a0_hbm, a0), (a1_hbm, a1))
        )
    ]
    for load in loads:
        load.start()

    barrier = pltpu.get_barrier_semaphore()
    for k in range(1, n):
        pl.semaphore_signal(barrier, inc=1, device_id=(z, lax.rem(me + k, n)), device_id_type=MESH)
    for k in range(1, reps):
        pl.semaphore_signal(barrier, inc=1, device_id=(lax.rem(z + k, reps), me), device_id_type=MESH)
    bt0[...] = b0[...].T
    bt1[...] = b1[...].T
    kept = [pltpu.make_async_copy(cots[p], gathered[p].at[me], load_sem.at[4 + p]) for p in range(2)]
    for copy in kept:
        copy.start()
    pl.semaphore_wait(barrier, n - 1 + reps - 1)

    def remote(src, dst, ss, rsem, target):
        return pltpu.make_async_remote_copy(
            src_ref=src, dst_ref=dst, send_sem=ss, recv_sem=rsem,
            device_id=target, device_id_type=MESH,
        )

    def shard_peer(k):
        return (z, lax.rem(me + k, n))

    def dp_peer(k):
        return (lax.rem(z + k, reps), me)

    def start(copies):
        for copy in copies:
            copy.start()
        return copies

    def arrived(copies):
        for copy in copies:
            copy.wait_recv()

    def scatter(src, dst, ss, rsem):
        return start([
            remote(src.at[lax.rem(me + k, n)], dst.at[k - 1], ss.at[k - 1], rsem.at[k - 1], shard_peer(k))
            for k in range(1, n)
        ])

    def spread(buf, ss, rsem):
        return start([
            remote(buf.at[me], buf.at[me], ss.at[k - 1], rsem.at[k - 1], shard_peer(k))
            for k in range(1, n)
        ])

    def total(own, parts, count):
        value = own
        for k in range(count):
            value = value + parts[k].astype(jnp.float32)
        return value

    def own_rows(buf):
        rows = buf.shape[0] // reps
        return pl.ds(pl.multiple_of(z * rows, rows), rows)

    def dp_scatter(src, dst, ss, rsem):
        rows = src.shape[0] // reps
        return start([
            remote(
                src.at[pl.ds(pl.multiple_of(lax.rem(z + k, reps) * rows, rows), rows)],
                dst.at[k - 1], ss.at[k - 1], rsem.at[k - 1], dp_peer(k),
            )
            for k in range(1, reps)
        ])

    def dp_spread(buf, ss, rsem):
        mine = own_rows(buf)
        return start([
            remote(buf.at[mine], buf.at[mine], ss.at[k - 1], rsem.at[k - 1], dp_peer(k))
            for k in range(1, reps)
        ])

    c = lax.rem(me, 2)
    x = lax.rem(me // 2, 2)
    y = me // 4
    at_c = me + 1 - 2 * c
    at_x = me + 2 - 4 * x
    at_y = me + 4 - 8 * y
    at_d = at_x + 4 - 8 * y
    pending = []

    token_piece = ps.shape[2]
    for p in range(2):
        value = mxu(sloc[p], cots[p][...], NN).astype(jnp.bfloat16)
        for j in range(n):
            ps[j, rank * p : rank * (p + 1), :] = value[:, j * token_piece : (j + 1) * token_piece]
    sent = scatter(ps, pr, ps_s, ps_r)
    pending += sent

    own = []
    for p in range(2):
        for i, target in enumerate((at_x, at_y, at_c)):
            own.append(remote(
                cots[p], gathered[p].at[me], own_send.at[3 * p + i], own_recv.at[3 * p + i], (z, target)
            ))
    start(own[:3])
    pending += own

    forwards, to_core = [], []

    def forward(p):
        own[3 * p].wait_recv()
        own[3 * p + 1].wait_recv()
        top, low = pl.ds(0, half), pl.ds(half, half)
        via_y = gathered[p].at[at_x, top]
        via_x = gathered[p].at[at_y, low]
        forwards.extend(start([
            remote(via_y, via_y, fwd_send.at[2 * p], fwd_recv.at[2 * p], (z, at_y)),
            remote(via_x, via_x, fwd_send.at[2 * p + 1], fwd_recv.at[2 * p + 1], (z, at_x)),
        ]))
        to_core.extend(start([
            remote(gathered[p].at[at_x], gathered[p].at[at_x], core_send.at[4 * p], core_recv.at[4 * p], (z, at_c)),
            remote(gathered[p].at[at_y], gathered[p].at[at_y], core_send.at[4 * p + 1], core_recv.at[4 * p + 1], (z, at_c)),
        ]))

    loads[0].wait()
    loads[1].wait()
    prior = [mxu(st[p], errs[p][...], NT) for p in range(2)]

    arrived(sent)
    pf[me] = total(ps[me].astype(jnp.float32), pr, n - 1).astype(jnp.bfloat16)
    sent = spread(pf, pg_s, pg_r)
    pending += sent
    loads[2].wait()
    loads[3].wait()
    arrived(sent)
    for p in range(2):
        value = jnp.concatenate([pf[j, rank * p : rank * (p + 1), :] for j in range(n)], axis=1)
        ls[rank * p : rank * (p + 1), :] = mxu(value, acts[p][...], NN) + prior[p]
    sent = dp_scatter(ls, lr, ls_s, ls_r)
    start(own[3:])
    pending += sent
    at0[...] = a0[...].T
    arrived(sent)
    mine = own_rows(ls)
    lf[mine, :] = total(ls[mine, :], lr, reps - 1) * (1.0 / reps)
    sent = dp_spread(lf, lg_s, lg_r)
    pending += sent
    at1[...] = a1[...].T
    forward(0)
    arrived(sent)

    lefts = [lf[rank * p : rank * (p + 1), :] for p in range(2)]
    for p in range(2):
        value = split_dot(lefts[p], acts[p][...], NT).astype(jnp.bfloat16)
        for j in range(n):
            qs[j, rank * p : rank * (p + 1), :] = value[:, j * token_piece : (j + 1) * token_piece]
    q_sent = scatter(qs, qr, qs_s, qs_r)
    gs[...] = jnp.zeros_like(gs)
    for p in range(2):
        gs[:, rank * p : rank * (p + 1)] = lax.dot_general(
            lefts[p], lefts[p], NT, precision=HIGH, preferred_element_type=jnp.float32
        )
    g_sent = start([
        remote(gs, gr.at[k - 1], gs_s.at[k - 1], gs_r.at[k - 1], shard_peer(k)) for k in range(1, n)
    ])
    cols = bt0.shape[0]
    for p in range(2):
        value = split_dot(lefts[p], errs[p][...], NN).astype(jnp.bfloat16)
        for j in range(n):
            ts[j, :, cols * p : cols * (p + 1)] = value[:, j * cols : (j + 1) * cols]
    t_sent = scatter(ts, tr, ts_s, ts_r)
    pending += q_sent + g_sent + t_sent

    arrived(q_sent)
    qf[me] = total(qs[me].astype(jnp.float32), qr, n - 1).astype(jnp.bfloat16)
    sent = spread(qf, qg_s, qg_r)
    pending += sent

    forward(1)

    arrived(sent)
    arrived(t_sent)
    for p in range(2):
        value = jnp.concatenate([qf[j, rank * p : rank * (p + 1), :] for j in range(n)], axis=1)
        rs[:, cols * p : cols * (p + 1)] = mxu(value, cots[p][...], NT)
    rs[...] = total(rs[...] + ts[me].astype(jnp.float32), tr, n - 1)
    sent = dp_scatter(rs, rr, rs_s, rs_r)
    pending += sent
    arrived(g_sent)
    gram = total(gs[...], gr, n - 1)
    grams = [gram[:, rank * p : rank * (p + 1)] for p in range(2)]
    for p in range(2):
        lg[rank * p : rank * (p + 1), :] = lax.dot_general(
            spd_inverse(grams[p]), lefts[p], NN, precision=HIGH, preferred_element_type=jnp.float32
        )
    arrived(sent)
    mine = own_rows(rs)
    rd[mine, :] = total(rs[mine, :], rr, reps - 1) * (1.0 / reps)
    sent = dp_spread(rd, rg_s, rg_r)
    pending += sent
    arrived(sent)
    rf[me] = rd[...].astype(jnp.bfloat16)
    sent = spread(rf, rf_s, rf_r)
    pending += sent
    for p in range(2):
        forwards[2 * p].wait_recv()
        forwards[2 * p + 1].wait_recv()
        top, low = pl.ds(0, half), pl.ds(half, half)
        to_core += start([
            remote(gathered[p].at[at_d, part], gathered[p].at[at_d, part],
                   core_send.at[4 * p + 2 + i], core_recv.at[4 * p + 2 + i], (z, at_c))
            for i, part in enumerate((top, low))
        ])
    arrived(sent)
    for j in range(n):
        for p in range(2):
            right[rank * p : rank * (p + 1), cols * j : cols * (j + 1)] = rf[j, :, cols * p : cols * (p + 1)]
    arrived(to_core)
    own[2].wait_recv()
    own[5].wait_recv()
    for copy in pending + forwards + to_core:
        copy.wait_send()
    for copy in kept:
        copy.wait()


def final_kernel(steps, at0, at1, b0, b1, e0, e1, w0, w1, lg, right, e0_new, e1_new, w0_new, w1_new):
    rank = lg.shape[0] // 2
    step = pl.program_id(0)
    z = lax.axis_index("dp")

    def part(p, place, at, b, e, w, e_new, w_new):
        span, narrow = b.shape[0], w.shape[1]
        rows = slice(rank * p, rank * (p + 1))
        left = two_terms(lg[rows, :])

        def approx(start, size):
            block = right[rows, pl.ds(pl.multiple_of(start, 128), size)]
            return mxu(left, jnp.concatenate([block, block], axis=0), TN)

        full = mxu(at[...], b[...], NT) + e[0].astype(jnp.float32)
        e_new[0] = (full - approx(place * span, span)).astype(jnp.bfloat16)
        w_new[...] = w[...] - approx((z * steps + place) * narrow, narrow)

    @pl.when(step < steps)
    def _():
        part(0, step, at0, b0, e0, w0, e0_new, w0_new)

    @pl.when(step >= steps)
    def _():
        part(1, step - steps, at1, b1, e1, w1, e1_new, w1_new)


def fast_body(
    hidden_in, context_in, query_cotan, output_cotan,
    query_error, output_error, query_weight, output_weight, start_factors,
):
    n = lax.axis_size("shard")
    reps = lax.axis_size("dp")
    tok, width = hidden_in.shape
    cols = query_cotan.shape[1]
    dout = start_factors.shape[1]
    rank = start_factors.shape[2]
    f32, bf16 = jnp.float32, jnp.bfloat16
    st = jnp.swapaxes(start_factors, 1, 2)
    sloc = jnp.swapaxes(
        lax.dynamic_slice_in_dim(start_factors, lax.axis_index("shard") * cols, cols, 1), 1, 2
    )
    any_spec = pl.BlockSpec(memory_space=pl.ANY)
    vmem = pl.BlockSpec(memory_space=pltpu.VMEM)
    dma = pltpu.SemaphoreType.DMA
    piece = tok // n
    wide = 2 * rank
    rows = wide // reps
    pair = 2 * cols
    g0, g1, at0, at1, lg, right = pl.pallas_call(
        functools.partial(chain_kernel, n, reps),
        out_shape=(
            jax.ShapeDtypeStruct((n, cols, tok), bf16),
            jax.ShapeDtypeStruct((n, cols, tok), bf16),
            jax.ShapeDtypeStruct((width, tok), bf16),
            jax.ShapeDtypeStruct((width, tok), bf16),
            jax.ShapeDtypeStruct((wide, width), f32),
            jax.ShapeDtypeStruct((wide, dout), bf16),
        ),
        in_specs=[any_spec, any_spec, vmem, vmem, any_spec, any_spec, vmem, vmem],
        out_specs=(any_spec, any_spec, vmem, vmem, vmem, vmem),
        scratch_shapes=[
            pltpu.VMEM((cols, tok), bf16),
            pltpu.VMEM((cols, tok), bf16),
            pltpu.VMEM((n, rank, pair), bf16),
            pltpu.VMEM((tok, width), bf16),
            pltpu.VMEM((tok, width), bf16),
            pltpu.VMEM((width, dout), bf16),
            pltpu.VMEM((width, dout), bf16),
            pltpu.VMEM((n, wide, piece), bf16),
            pltpu.VMEM((n - 1, wide, piece), bf16),
            pltpu.VMEM((n, wide, piece), bf16),
            pltpu.VMEM((wide, width), f32),
            pltpu.VMEM((reps - 1, rows, width), f32),
            pltpu.VMEM((wide, width), f32),
            pltpu.VMEM((n, wide, piece), bf16),
            pltpu.VMEM((n - 1, wide, piece), bf16),
            pltpu.VMEM((n, wide, piece), bf16),
            pltpu.VMEM((n, rank, pair), bf16),
            pltpu.VMEM((n - 1, rank, pair), bf16),
            pltpu.VMEM((rank, 128), f32),
            pltpu.VMEM((n - 1, rank, 128), f32),
            pltpu.VMEM((rank, pair), f32),
            pltpu.VMEM((reps - 1, rank // reps, pair), f32),
            pltpu.VMEM((rank, pair), f32),
            dma((6,)), dma((6,)), dma((6,)), dma((4,)), dma((4,)), dma((8,)), dma((8,)),
        ]
        + [dma((n - 1,))] * 4 + [dma((reps - 1,))] * 4
        + [dma((n - 1,))] * 8 + [dma((reps - 1,))] * 4 + [dma((n - 1,))] * 2,
        compiler_params=pltpu.CompilerParams(
            collective_id=0, has_side_effects=True, vmem_limit_bytes=48 * 1024 * 1024
        ),
    )(
        hidden_in, context_in, query_cotan, output_cotan,
        query_error[0], output_error[0], st, sloc,
    )

    span = dout // 5

    steps = dout // span
    narrow = query_weight.shape[1] // steps

    def first(i):
        return jnp.minimum(i, steps - 1)

    def second(i):
        return jnp.maximum(i - steps, 0)

    def whole(shape):
        return pl.BlockSpec(shape, lambda i: (0, 0))

    err_specs = [pl.BlockSpec((1, width, span), lambda i, at=at: (0, 0, at(i))) for at in (first, second)]
    w_specs = [pl.BlockSpec((width, narrow), lambda i, at=at: (0, at(i))) for at in (first, second)]
    b_specs = [pl.BlockSpec((span, tok), lambda i, at=at: (at(i), 0)) for at in (first, second)]
    outs = (query_error, output_error, query_weight, output_weight)
    return pl.pallas_call(
        functools.partial(final_kernel, steps),
        grid=(2 * steps,),
        in_specs=[whole((width, tok))] * 2 + b_specs + err_specs + w_specs
        + [whole((wide, width)), whole((wide, dout))],
        out_specs=tuple(err_specs + w_specs),
        out_shape=tuple(jax.ShapeDtypeStruct(out.shape, out.dtype) for out in outs),
        compiler_params=pltpu.CompilerParams(vmem_limit_bytes=48 * 1024 * 1024),
    )(
        at0, at1, g0.reshape(dout, tok), g1.reshape(dout, tok),
        query_error, output_error, query_weight, output_weight, lg, right,
    )


def solution(mesh):
    placed = (
        P("dp", "shard"),
        P("dp", "shard"),
        P("dp", "shard"),
        P("dp", "shard"),
        P("dp", "shard", None),
        P("dp", "shard", None),
        P("shard", "dp"),
        P("shard", "dp"),
        P(),
    )
    return jax.shard_map(
        fast_body if mesh.shape["shard"] == 8 and mesh.shape["dp"] == 4 else body,
        mesh=mesh,
        in_specs=placed,
        out_specs=(
            P("dp", "shard", None),
            P("dp", "shard", None),
            P("shard", "dp"),
            P("shard", "dp"),
        ),
        check_vma=False,
    )
```

```python
import functools

import jax
import jax.numpy as jnp
from jax import lax
from jax.experimental import pallas as pl
from jax.experimental.pallas import tpu as pltpu
from jax.sharding import PartitionSpec as P

HIGH = lax.Precision.HIGHEST


def contract_tokens(left_op, right_op):
    return lax.dot_general(
        left_op, right_op, (((0,), (0,)), ((), ())), preferred_element_type=jnp.float32
    )


def form_grads(hidden_in, context_in, query_cotan, output_cotan):

    def query_part(piece, start):
        return contract_tokens(hidden_in, piece)

    def output_part(piece, start):
        return contract_tokens(context_in, piece)

    query_grad = query_part(lax.all_gather(query_cotan, "shard", axis=1, tiled=True), jnp.int32(0))
    output_grad = output_part(
        lax.all_gather(output_cotan, "shard", axis=1, tiled=True), jnp.int32(0)
    )
    return (query_grad, output_grad)


def orthonormal(left, gram):
    chol = jnp.linalg.cholesky(gram)
    return lax.linalg.triangular_solve(chol, left, left_side=False, lower=True, transpose_a=True)


def body(
    hidden_in,
    context_in,
    query_cotan,
    output_cotan,
    query_error,
    output_error,
    query_weight,
    output_weight,
    start_factors,
):
    replicas = lax.axis_size("dp")
    query_start = start_factors[0].astype(jnp.float32)
    output_start = start_factors[1].astype(jnp.float32)
    query_prior = query_error[0].astype(jnp.float32)
    output_prior = output_error[0].astype(jnp.float32)
    query_grad, output_grad = form_grads(hidden_in, context_in, query_cotan, output_cotan)
    query_full = query_grad + query_prior
    output_full = output_grad + output_prior
    query_left = jnp.dot(query_full, query_start, precision=HIGH)
    output_left = jnp.dot(output_full, output_start, precision=HIGH)
    query_left, output_left = lax.psum((query_left, output_left), "dp")
    query_left = query_left / jnp.float32(replicas)
    output_left = output_left / jnp.float32(replicas)
    query_gram, output_gram = lax.psum(
        (
            jnp.dot(query_left.T, query_left, precision=HIGH),
            jnp.dot(output_left.T, output_left, precision=HIGH),
        ),
        "shard",
    )
    query_ortho = orthonormal(query_left, query_gram)
    output_ortho = orthonormal(output_left, output_gram)
    query_term = jnp.dot(query_full.T, query_ortho, precision=HIGH)
    output_term = jnp.dot(output_full.T, output_ortho, precision=HIGH)
    query_part, output_part = (
        lax.psum_scatter(
            query_term.astype(jnp.bfloat16), "shard", scatter_dimension=0, tiled=True
        ).astype(jnp.float32),
        lax.psum_scatter(
            output_term.astype(jnp.bfloat16), "shard", scatter_dimension=0, tiled=True
        ).astype(jnp.float32),
    )
    query_part, output_part = lax.psum((query_part, output_part), "dp")
    query_right, output_right = (
        lax.all_gather(query_part, "shard", axis=0, tiled=True),
        lax.all_gather(output_part, "shard", axis=0, tiled=True),
    )
    query_right = query_right / jnp.float32(replicas)
    output_right = output_right / jnp.float32(replicas)
    query_approx = jnp.dot(query_ortho, query_right.T, precision=HIGH)
    output_approx = jnp.dot(output_ortho, output_right.T, precision=HIGH)
    query_error_new = (query_full - query_approx).astype(jnp.bfloat16)[None]
    output_error_new = (output_full - output_approx).astype(jnp.bfloat16)[None]
    weight_cols = query_weight.shape[1]
    col_start = lax.axis_index("dp") * weight_cols
    query_cols = lax.dynamic_slice_in_dim(query_approx, col_start, weight_cols, 1)
    output_cols = lax.dynamic_slice_in_dim(output_approx, col_start, weight_cols, 1)
    return (
        query_error_new,
        output_error_new,
        query_weight - query_cols,
        output_weight - output_cols,
    )


NT = (((1,), (1,)), ((), ()))
NN = (((1,), (0,)), ((), ()))
TN = (((0,), (0,)), ((), ()))
MESH = pl.DeviceIdType.MESH


def mxu(lhs, rhs, dims):
    return lax.dot_general(lhs, rhs, dims, preferred_element_type=jnp.float32)


def two_terms(value):
    high = value.astype(jnp.bfloat16)
    low = (value - high.astype(jnp.float32)).astype(jnp.bfloat16)
    return jnp.concatenate([high, low], axis=0)


def split_dot(value, rhs, dims):
    rows = value.shape[0]
    both = mxu(two_terms(value), rhs, dims)
    return both[:rows] + both[rows:]


def spd_inverse(gram):
    size = gram.shape[0]
    row_id = lax.broadcasted_iota(jnp.int32, (size, size), 0)
    col_id = lax.broadcasted_iota(jnp.int32, (size, size), 1)
    value = gram
    for k in range(size):
        row = value[k : k + 1, :]
        col = value[:, k : k + 1]
        inv = 1.0 / value[k : k + 1, k : k + 1]
        scaled = row * inv
        rest = value - col * scaled
        rest = jnp.where(col_id == k, -col * inv, rest)
        value = jnp.where(row_id == k, jnp.where(col_id == k, inv, scaled), rest)
    return value


def chain_kernel(
    n, reps,
    a0_hbm, a1_hbm, b0, b1, e0_hbm, e1_hbm, st, sloc,
    g0, g1, at0, at1, lg, right,
    bt0, bt1, rf, a0, a1, e0, e1, ps, pr, pf, ls, lr, lf, qs, qr, qf, ts, tr, gs, gr, rs, rr, rd,
    load_sem, own_send, own_recv, fwd_send, fwd_recv, core_send, core_recv,
    ps_s, ps_r, pg_s, pg_r, ls_s, ls_r, lg_s, lg_r,
    qs_s, qs_r, qg_s, qg_r, ts_s, ts_r, gs_s, gs_r,
    rs_s, rs_r, rg_s, rg_r, rf_s, rf_r,
):
    me = lax.axis_index("shard")
    z = lax.axis_index("dp")
    rank = st.shape[1]
    acts, errs, cots, gathered = (a0, a1), (e0, e1), (bt0, bt1), (g0, g1)
    half = b0.shape[1] // 2

    loads = [
        pltpu.make_async_copy(src, dst, load_sem.at[i])
        for i, (src, dst) in enumerate(
            ((e0_hbm, e0), (e1_hbm, e1), (a0_hbm, a0), (a1_hbm, a1))
        )
    ]
    for load in loads:
        load.start()

    barrier = pltpu.get_barrier_semaphore()
    for k in range(1, n):
        pl.semaphore_signal(barrier, inc=1, device_id=(z, lax.rem(me + k, n)), device_id_type=MESH)
    for k in range(1, reps):
        pl.semaphore_signal(barrier, inc=1, device_id=(lax.rem(z + k, reps), me), device_id_type=MESH)
    bt0[...] = b0[...].T
    bt1[...] = b1[...].T
    kept = [pltpu.make_async_copy(cots[p], gathered[p].at[me], load_sem.at[4 + p]) for p in range(2)]
    for copy in kept:
        copy.start()
    pl.semaphore_wait(barrier, n - 1 + reps - 1)

    def remote(src, dst, ss, rsem, target):
        return pltpu.make_async_remote_copy(
            src_ref=src, dst_ref=dst, send_sem=ss, recv_sem=rsem,
            device_id=target, device_id_type=MESH,
        )

    def shard_peer(k):
        return (z, lax.rem(me + k, n))

    def dp_peer(k):
        return (lax.rem(z + k, reps), me)

    def start(copies):
        for copy in copies:
            copy.start()
        return copies

    def arrived(copies):
        for copy in copies:
            copy.wait_recv()

    def scatter(src, dst, ss, rsem):
        return start([
            remote(src.at[lax.rem(me + k, n)], dst.at[k - 1], ss.at[k - 1], rsem.at[k - 1], shard_peer(k))
            for k in range(1, n)
        ])

    def spread(buf, ss, rsem):
        return start([
            remote(buf.at[me], buf.at[me], ss.at[k - 1], rsem.at[k - 1], shard_peer(k))
            for k in range(1, n)
        ])

    def total(own, parts, count):
        value = own
        for k in range(count):
            value = value + parts[k].astype(jnp.float32)
        return value

    def own_rows(buf):
        rows = buf.shape[0] // reps
        return pl.ds(pl.multiple_of(z * rows, rows), rows)

    def dp_scatter(src, dst, ss, rsem):
        rows = src.shape[0] // reps
        return start([
            remote(
                src.at[pl.ds(pl.multiple_of(lax.rem(z + k, reps) * rows, rows), rows)],
                dst.at[k - 1], ss.at[k - 1], rsem.at[k - 1], dp_peer(k),
            )
            for k in range(1, reps)
        ])

    def dp_spread(buf, ss, rsem):
        mine = own_rows(buf)
        return start([
            remote(buf.at[mine], buf.at[mine], ss.at[k - 1], rsem.at[k - 1], dp_peer(k))
            for k in range(1, reps)
        ])

    c = lax.rem(me, 2)
    x = lax.rem(me // 2, 2)
    y = me // 4
    at_c = me + 1 - 2 * c
    at_x = me + 2 - 4 * x
    at_y = me + 4 - 8 * y
    at_d = at_x + 4 - 8 * y
    pending = []

    token_piece = ps.shape[2]
    for p in range(2):
        value = mxu(sloc[p], cots[p][...], NN).astype(jnp.bfloat16)
        for j in range(n):
            ps[j, rank * p : rank * (p + 1), :] = value[:, j * token_piece : (j + 1) * token_piece]
    sent = scatter(ps, pr, ps_s, ps_r)
    pending += sent

    own = []
    for p in range(2):
        for i, target in enumerate((at_x, at_y, at_c)):
            own.append(remote(
                cots[p], gathered[p].at[me], own_send.at[3 * p + i], own_recv.at[3 * p + i], (z, target)
            ))
    start(own[:3])
    pending += own

    forwards, to_core = [], []

    def forward(p):
        own[3 * p].wait_recv()
        own[3 * p + 1].wait_recv()
        top, low = pl.ds(0, half), pl.ds(half, half)
        via_y = gathered[p].at[at_x, top]
        via_x = gathered[p].at[at_y, low]
        forwards.extend(start([
            remote(via_y, via_y, fwd_send.at[2 * p], fwd_recv.at[2 * p], (z, at_y)),
            remote(via_x, via_x, fwd_send.at[2 * p + 1], fwd_recv.at[2 * p + 1], (z, at_x)),
        ]))
        to_core.extend(start([
            remote(gathered[p].at[at_x], gathered[p].at[at_x], core_send.at[4 * p], core_recv.at[4 * p], (z, at_c)),
            remote(gathered[p].at[at_y], gathered[p].at[at_y], core_send.at[4 * p + 1], core_recv.at[4 * p + 1], (z, at_c)),
        ]))

    loads[0].wait()
    loads[1].wait()
    prior = [mxu(st[p], errs[p][...], NT) for p in range(2)]

    arrived(sent)
    pf[me] = total(ps[me].astype(jnp.float32), pr, n - 1).astype(jnp.bfloat16)
    sent = spread(pf, pg_s, pg_r)
    pending += sent
    loads[2].wait()
    loads[3].wait()
    arrived(sent)
    for p in range(2):
        value = jnp.concatenate([pf[j, rank * p : rank * (p + 1), :] for j in range(n)], axis=1)
        ls[rank * p : rank * (p + 1), :] = (mxu(value, acts[p][...], NN) + prior[p]).astype(jnp.bfloat16)
    sent = dp_scatter(ls, lr, ls_s, ls_r)
    start(own[3:])
    pending += sent
    at0[...] = a0[...].T
    arrived(sent)
    mine = own_rows(ls)
    lf[mine, :] = (total(ls[mine, :].astype(jnp.float32), lr, reps - 1) * (1.0 / reps)).astype(jnp.bfloat16)
    sent = dp_spread(lf, lg_s, lg_r)
    pending += sent
    at1[...] = a1[...].T
    forward(0)
    arrived(sent)

    lefts = [lf[rank * p : rank * (p + 1), :] for p in range(2)]
    for p in range(2):
        value = mxu(lefts[p], acts[p][...], NT).astype(jnp.bfloat16)
        for j in range(n):
            qs[j, rank * p : rank * (p + 1), :] = value[:, j * token_piece : (j + 1) * token_piece]
    q_sent = scatter(qs, qr, qs_s, qs_r)
    gs[...] = jnp.zeros_like(gs)
    for p in range(2):
        gs[:, rank * p : rank * (p + 1)] = mxu(lefts[p], lefts[p], NT)
    g_sent = start([
        remote(gs, gr.at[k - 1], gs_s.at[k - 1], gs_r.at[k - 1], shard_peer(k)) for k in range(1, n)
    ])
    cols = bt0.shape[0]
    for p in range(2):
        value = mxu(lefts[p], errs[p][...], NN).astype(jnp.bfloat16)
        for j in range(n):
            ts[j, :, cols * p : cols * (p + 1)] = value[:, j * cols : (j + 1) * cols]
    t_sent = scatter(ts, tr, ts_s, ts_r)
    pending += q_sent + g_sent + t_sent

    arrived(q_sent)
    qf[me] = total(qs[me].astype(jnp.float32), qr, n - 1).astype(jnp.bfloat16)
    sent = spread(qf, qg_s, qg_r)
    pending += sent

    forward(1)

    arrived(sent)
    arrived(t_sent)
    for p in range(2):
        value = jnp.concatenate([qf[j, rank * p : rank * (p + 1), :] for j in range(n)], axis=1)
        rs[:, cols * p : cols * (p + 1)] = mxu(value, cots[p][...], NT)
    rs[...] = total(rs[...] + ts[me].astype(jnp.float32), tr, n - 1)
    sent = dp_scatter(rs, rr, rs_s, rs_r)
    pending += sent
    arrived(g_sent)
    gram = total(gs[...], gr, n - 1)
    grams = [gram[:, rank * p : rank * (p + 1)] for p in range(2)]
    for p in range(2):
        lg[rank * p : rank * (p + 1), :] = lax.dot_general(
            spd_inverse(grams[p]), lefts[p].astype(jnp.float32), NN, precision=HIGH, preferred_element_type=jnp.float32
        )
    arrived(sent)
    mine = own_rows(rs)
    rd[mine, :] = total(rs[mine, :], rr, reps - 1) * (1.0 / reps)
    sent = dp_spread(rd, rg_s, rg_r)
    pending += sent
    arrived(sent)
    rf[me] = rd[...].astype(jnp.bfloat16)
    sent = spread(rf, rf_s, rf_r)
    pending += sent
    for p in range(2):
        forwards[2 * p].wait_recv()
        forwards[2 * p + 1].wait_recv()
        top, low = pl.ds(0, half), pl.ds(half, half)
        to_core += start([
            remote(gathered[p].at[at_d, part], gathered[p].at[at_d, part],
                   core_send.at[4 * p + 2 + i], core_recv.at[4 * p + 2 + i], (z, at_c))
            for i, part in enumerate((top, low))
        ])
    arrived(sent)
    for j in range(n):
        for p in range(2):
            right[rank * p : rank * (p + 1), cols * j : cols * (j + 1)] = rf[j, :, cols * p : cols * (p + 1)]
    arrived(to_core)
    own[2].wait_recv()
    own[5].wait_recv()
    for copy in pending + forwards + to_core:
        copy.wait_send()
    for copy in kept:
        copy.wait()


def final_kernel(steps, at0, at1, b0, b1, e0, e1, w0, w1, lg, right, e0_new, e1_new, w0_new, w1_new):
    rank = lg.shape[0] // 2
    step = pl.program_id(0)
    z = lax.axis_index("dp")

    def part(p, place, at, b, e, w, e_new, w_new):
        span, narrow = b.shape[0], w.shape[1]
        rows = slice(rank * p, rank * (p + 1))
        left = two_terms(lg[rows, :])

        def approx(start, size):
            block = right[rows, pl.ds(pl.multiple_of(start, 128), size)]
            return mxu(left, jnp.concatenate([block, block], axis=0), TN)

        full = mxu(at[...], b[...], NT) + e[0].astype(jnp.float32)
        e_new[0] = (full - approx(place * span, span)).astype(jnp.bfloat16)
        w_new[...] = w[...] - approx((z * steps + place) * narrow, narrow)

    @pl.when(step < steps)
    def _():
        part(0, step, at0, b0, e0, w0, e0_new, w0_new)

    @pl.when(step >= steps)
    def _():
        part(1, step - steps, at1, b1, e1, w1, e1_new, w1_new)


def fast_body(
    hidden_in, context_in, query_cotan, output_cotan,
    query_error, output_error, query_weight, output_weight, start_factors,
):
    n = lax.axis_size("shard")
    reps = lax.axis_size("dp")
    tok, width = hidden_in.shape
    cols = query_cotan.shape[1]
    dout = start_factors.shape[1]
    rank = start_factors.shape[2]
    f32, bf16 = jnp.float32, jnp.bfloat16
    st = jnp.swapaxes(start_factors, 1, 2)
    sloc = jnp.swapaxes(
        lax.dynamic_slice_in_dim(start_factors, lax.axis_index("shard") * cols, cols, 1), 1, 2
    )
    any_spec = pl.BlockSpec(memory_space=pl.ANY)
    vmem = pl.BlockSpec(memory_space=pltpu.VMEM)
    dma = pltpu.SemaphoreType.DMA
    piece = tok // n
    wide = 2 * rank
    rows = wide // reps
    pair = 2 * cols
    g0, g1, at0, at1, lg, right = pl.pallas_call(
        functools.partial(chain_kernel, n, reps),
        out_shape=(
            jax.ShapeDtypeStruct((n, cols, tok), bf16),
            jax.ShapeDtypeStruct((n, cols, tok), bf16),
            jax.ShapeDtypeStruct((width, tok), bf16),
            jax.ShapeDtypeStruct((width, tok), bf16),
            jax.ShapeDtypeStruct((wide, width), f32),
            jax.ShapeDtypeStruct((wide, dout), bf16),
        ),
        in_specs=[any_spec, any_spec, vmem, vmem, any_spec, any_spec, vmem, vmem],
        out_specs=(any_spec, any_spec, vmem, vmem, vmem, vmem),
        scratch_shapes=[
            pltpu.VMEM((cols, tok), bf16),
            pltpu.VMEM((cols, tok), bf16),
            pltpu.VMEM((n, rank, pair), bf16),
            pltpu.VMEM((tok, width), bf16),
            pltpu.VMEM((tok, width), bf16),
            pltpu.VMEM((width, dout), bf16),
            pltpu.VMEM((width, dout), bf16),
            pltpu.VMEM((n, wide, piece), bf16),
            pltpu.VMEM((n - 1, wide, piece), bf16),
            pltpu.VMEM((n, wide, piece), bf16),
            pltpu.VMEM((wide, width), bf16),
            pltpu.VMEM((reps - 1, rows, width), bf16),
            pltpu.VMEM((wide, width), bf16),
            pltpu.VMEM((n, wide, piece), bf16),
            pltpu.VMEM((n - 1, wide, piece), bf16),
            pltpu.VMEM((n, wide, piece), bf16),
            pltpu.VMEM((n, rank, pair), bf16),
            pltpu.VMEM((n - 1, rank, pair), bf16),
            pltpu.VMEM((rank, 128), f32),
            pltpu.VMEM((n - 1, rank, 128), f32),
            pltpu.VMEM((rank, pair), f32),
            pltpu.VMEM((reps - 1, rank // reps, pair), f32),
            pltpu.VMEM((rank, pair), f32),
            dma((6,)), dma((6,)), dma((6,)), dma((4,)), dma((4,)), dma((8,)), dma((8,)),
        ]
        + [dma((n - 1,))] * 4 + [dma((reps - 1,))] * 4
        + [dma((n - 1,))] * 8 + [dma((reps - 1,))] * 4 + [dma((n - 1,))] * 2,
        compiler_params=pltpu.CompilerParams(
            collective_id=0, has_side_effects=True, vmem_limit_bytes=48 * 1024 * 1024
        ),
    )(
        hidden_in, context_in, query_cotan, output_cotan,
        query_error[0], output_error[0], st, sloc,
    )

    span = dout // 5

    steps = dout // span
    narrow = query_weight.shape[1] // steps

    def first(i):
        return jnp.minimum(i, steps - 1)

    def second(i):
        return jnp.maximum(i - steps, 0)

    def whole(shape):
        return pl.BlockSpec(shape, lambda i: (0, 0))

    err_specs = [pl.BlockSpec((1, width, span), lambda i, at=at: (0, 0, at(i))) for at in (first, second)]
    w_specs = [pl.BlockSpec((width, narrow), lambda i, at=at: (0, at(i))) for at in (first, second)]
    b_specs = [pl.BlockSpec((span, tok), lambda i, at=at: (at(i), 0)) for at in (first, second)]
    outs = (query_error, output_error, query_weight, output_weight)
    return pl.pallas_call(
        functools.partial(final_kernel, steps),
        grid=(2 * steps,),
        in_specs=[whole((width, tok))] * 2 + b_specs + err_specs + w_specs
        + [whole((wide, width)), whole((wide, dout))],
        out_specs=tuple(err_specs + w_specs),
        out_shape=tuple(jax.ShapeDtypeStruct(out.shape, out.dtype) for out in outs),
        compiler_params=pltpu.CompilerParams(vmem_limit_bytes=48 * 1024 * 1024),
    )(
        at0, at1, g0.reshape(dout, tok), g1.reshape(dout, tok),
        query_error, output_error, query_weight, output_weight, lg, right,
    )


def solution(mesh):
    placed = (
        P("dp", "shard"),
        P("dp", "shard"),
        P("dp", "shard"),
        P("dp", "shard"),
        P("dp", "shard", None),
        P("dp", "shard", None),
        P("shard", "dp"),
        P("shard", "dp"),
        P(),
    )
    return jax.shard_map(
        fast_body if mesh.shape["shard"] == 8 and mesh.shape["dp"] == 4 else body,
        mesh=mesh,
        in_specs=placed,
        out_specs=(
            P("dp", "shard", None),
            P("dp", "shard", None),
            P("shard", "dp"),
            P("shard", "dp"),
        ),
        check_vma=False,
    )
```
